32 devices in a mesh: row: 8 (over z, y), col: 4 (over x, core).
Axes of the slice: x: 2, y: 2, z: 4, core: 2. Of those that a mesh axis runs over, the one named last changes fastest.
Arguments:
- density: float32 [2, 160, 32, 160, 160], P(None, 'col', None, 'row'), may hold values from -2 to 2
- potential: float32 [160, 160], P('row'), may hold values from 0 to 2
Outputs:
- liouville: float32 [2, 160, 160, 1024], P(None, 'col', 'row')
The draws below stay inside these ranges and needn't reach their ends.
All inputs are finite; a program needn't handle non-finite values.
Results may differ from the reference program's by a relative error of at most 0.000055.
Values sent between devices are 32-bit elements; how exact they have to be, the bound alone decides.
A program may use at most 384 MiB of HBM per device.

```python
import jax
import jax.numpy as jnp
from jax import lax

G = 160
S = 32


def block_levels(key, shape, cuts, smallest, high):
    loudness, own = 1.0, jax.random.fold_in(key, 6)
    for axis_at, shards_of in cuts:
        draws = jnp.exp(jax.random.uniform(jax.random.fold_in(own, axis_at), (shards_of,), jnp.float32, smallest / len(cuts), high / len(cuts)))
        loudness = loudness * jnp.repeat(draws, shape[axis_at] // shards_of).reshape([-1 if axis == axis_at else 1 for axis in range(len(shape))])
    return loudness


def normal_values(stream_key, dims, deviation, bound, cuts=(), held_as=jnp.bfloat16):
    array = jax.random.normal(stream_key, dims, jnp.float32) * deviation
    if len(cuts) > 0:
        array = block_levels(stream_key, dims, cuts, -0.22, 0.18) * array
    return jnp.clip(array, min=-bound, max=bound).astype(held_as)


def setup_inputs(seed: int = 0) -> dict:
    seeds = jax.random.split(jax.random.key(seed), 3)
    return {
        "density": normal_values(seeds[0], (2, G, S, G, G), 0.3, 2.0, ((1, 4), (3, 8)), jnp.float32),
        "potential": jnp.clip(2.0 * jax.random.uniform(seeds[1], (G, G), jnp.float32) ** block_levels(seeds[1], (G, G), ((0, 8),), -0.2, 0.2), 0.0, 2.0),
    }


friction = 0.005
diffusion = 0.0001


def spectral(values, factor, along):
    shape = [1] * values.ndim
    shape[along] = factor.shape[0]
    spectrum = jnp.fft.fft(values, axis=along) * factor.reshape(shape)
    return jnp.real(jnp.fft.ifft(spectrum, axis=along)).astype(values.dtype)


def reference(density, potential):
    grid_width = density.shape[3]
    window_size = density.shape[2]
    wavenumber = 2.0 * jnp.pi * jnp.fft.fftfreq(grid_width)
    kinetic_factor = 0.5 * wavenumber * wavenumber
    slope_wave = jnp.where(jnp.arange(grid_width) == grid_width // 2, 0.0, wavenumber)
    slope_factor = 1j * slope_wave
    offset_one = (jnp.arange(window_size)[None, :] - jnp.arange(window_size)[:, None]).astype(density.dtype)

    def single(column_pair):
        column, slab = column_pair
        window_part = slab[..., :window_size]
        applied = spectral(slab, kinetic_factor, 3)[..., :window_size] + spectral(slab, kinetic_factor, 2)[..., :window_size]
        applied = applied + potential[None, None, :, :window_size] * window_part
        grad_one = spectral(slab, slope_factor, 3)[..., :window_size]
        grad_two = spectral(slab, slope_factor, 2)[..., :window_size]
        offset_two = (jnp.arange(grid_width) - column).astype(density.dtype).reshape(1, 1, grid_width, 1)
        drift_sum = offset_one.reshape(1, window_size, 1, window_size) * grad_one + offset_two * grad_two
        real_part = applied[1] - friction * drift_sum[0]
        imag_part = -applied[0] - friction * drift_sum[1]
        return jnp.stack([real_part, imag_part])

    halfway = lax.map(single, (jnp.arange(grid_width), jnp.moveaxis(density, 1, 0)))
    mirrored = jnp.transpose(halfway, (3, 1, 4, 0, 2))
    window_part = jnp.moveaxis(density[..., :window_size], 1, 0)
    offset_rows = (jnp.arange(grid_width)[None, :] - jnp.arange(grid_width)[:, None]).astype(density.dtype)
    squared = offset_rows.reshape(grid_width, 1, grid_width, 1) ** 2 + offset_one.reshape(1, window_size, 1, window_size) ** 2
    real_out = halfway[:, 0] + mirrored[:, 0] - diffusion * squared * window_part[:, 0]
    imag_out = halfway[:, 1] - mirrored[:, 1] - diffusion * squared * window_part[:, 1]
    result = jnp.stack([real_out, imag_out])
    return jnp.transpose(result, (0, 1, 3, 2, 4)).reshape(2, grid_width, grid_width, window_size * window_size)
```

```python
import functools

import jax
import jax.numpy as jnp
import numpy as np
from jax import lax
from jax.experimental import pallas as pl
from jax.experimental.pallas import tpu as pltpu
from jax.sharding import PartitionSpec as P

friction = 0.005
diffusion = 0.0001
LANES = 128
VMEM = 56 * 2**20


def operators(grid_width):
    n = np.arange(grid_width)
    wave = 2.0 * np.pi * np.fft.fftfreq(grid_width)
    slope_wave = np.where(n == grid_width // 2, 0.0, wave)
    angles = 2.0 * np.pi / grid_width * (n[:, None] * n[None, :] % grid_width)
    kinetic_row = (0.5 * wave * wave * np.cos(angles)).sum(1) / grid_width
    slope_row = -(slope_wave * np.sin(angles)).sum(1) / grid_width
    distance = (n[:, None] - n[None, :]) % grid_width
    return kinetic_row[distance], slope_row[distance]


def split_host(matrix):
    high = matrix.astype(np.float32).astype(jnp.bfloat16)
    low = (matrix - high.astype(np.float64)).astype(np.float32).astype(jnp.bfloat16)
    return jnp.asarray(high), jnp.asarray(low)


def split(values):
    high = values.astype(jnp.bfloat16)
    return high, (values - high.astype(jnp.float32)).astype(jnp.bfloat16)


def dot(a, b):
    return jnp.dot(a, b, preferred_element_type=jnp.float32)


def up8(n):
    return (n + 7) // 8 * 8


def first_kernel(group, rows, d_ref, v_ref, high_ref, low_ref, eye_ref, w_ref, l_ref, pad):
    blocks, tall = pad.shape[0], pad.shape[1]

    @pl.when((pl.program_id(0) == 0) & (pl.program_id(1) == 0))
    def _():
        pad[...] = jnp.zeros_like(pad)

    window, mixed = [], []
    for c in range(2):
        win = jnp.zeros((blocks * tall, LANES), jnp.float32)
        mix = jnp.zeros((blocks * tall, 2 * LANES), jnp.float32)
        for q in range(group):
            pad[:, :rows, :] = d_ref[c, :, q]
            high, low = split(pad[...].reshape(blocks * tall, pad.shape[2]))
            mix += dot(high, high_ref[q]) + dot(low, high_ref[q]) + dot(high, low_ref[q])
            win += dot(high, eye_ref[q]) + dot(low, eye_ref[q])
        window.append(win.reshape(blocks, tall, LANES)[:, :rows])
        mixed.append(mix.reshape(blocks, tall, 2 * LANES)[:, :rows])
    v = v_ref[...][None]
    w_ref[0, 0] = window[0]
    w_ref[0, 1] = window[1]
    l_ref[0] = mixed[1][..., :LANES] + mixed[0][..., LANES:] + v * window[1]
    l_ref[1] = mixed[1][..., LANES:] - mixed[0][..., :LANES] - v * window[0]


def mirror_kernel(rows, l_ref, perm_ref, o_ref, pad, back):
    sign = 1.0 - 2.0 * pl.program_id(0).astype(jnp.float32)
    tall, lanes = pad.shape[1], pad.shape[2]
    quarters, wide = o_ref.shape[0], o_ref.shape[5]
    pad[...] = jnp.zeros_like(pad)
    for b in range(rows):
        pad[b, :rows, :] = l_ref[0, :, b, :]
    high, low = split(pad[...].reshape(rows * tall, lanes) * sign)
    for u in range(quarters):
        part = perm_ref[:, u * wide : (u + 1) * wide]
        out = dot(high, part) + dot(low, part)
        o_ref[u, 0, 0] = out.reshape(rows, tall, wide)[:, :rows]


def second_kernel(pieces, rows, tall, start_ref, *refs):
    parts = refs[:pieces]
    high_ref, low_ref, o_ref, pad = refs[pieces:]
    wide = pad.shape[2]

    @pl.when(pl.program_id(0) == 0)
    def _():
        pad[...] = jnp.zeros_like(pad)

    column = (start_ref[0] + pl.program_id(0)).astype(jnp.float32)
    out = []
    for c in range(2):
        for k in range(pieces):
            pad[c, k * tall : k * tall + rows, :] = parts[k][c, 0]
        high, low = split(pad[c])
        out.append(dot(high_ref[...], high) + dot(high_ref[...], low) + dot(low_ref[...], high))
    half = pieces * tall
    at = lax.broadcasted_iota(jnp.int32, (tall, wide), 0).astype(jnp.float32) - column
    for r in range(pieces):
        here = slice(r * tall, (r + 1) * tall)
        there = slice(half + r * tall, half + (r + 1) * tall)
        offset = friction * (at + float(r * rows))
        o_ref[r, 0, 0] = (out[1][here] - offset * out[0][there])[:rows]
        o_ref[r, 1, 0] = (-out[0][here] - offset * out[1][there])[:rows]


def last_kernel(quarters, ratio, rows, window, where_ref, y_ref, r_ref, w_ref, perm_ref, sq_ref, o_ref, pad):
    c, h = pl.program_id(0), pl.program_id(1)
    col, source, own, row_start, col_start = (where_ref[k] for k in range(5))
    sign = 1.0 - 2.0 * c.astype(jnp.float32)
    tall, wide = pad.shape[1], pad.shape[2]
    lanes = o_ref.shape[3]
    pad[...] = jnp.zeros_like(pad)
    total = jnp.zeros((rows * tall, lanes), jnp.float32)
    for u in range(quarters):
        s = lax.rem(col - u + quarters, quarters)
        for p in range(rows):
            pad[p, :rows, :] = y_ref[s, 0, 0, :, p, :]
        high, low = split(pad[...].reshape(rows * tall, wide) * sign)
        part = perm_ref[u * wide : (u + 1) * wide, :]
        total += dot(high, part) + dot(low, part)
    total = total.reshape(rows, tall, lanes)[:, :rows]
    b = row_start + lax.broadcasted_iota(jnp.int32, (rows, rows, 1), 1)
    p = col_start + h * rows + lax.broadcasted_iota(jnp.int32, (rows, rows, 1), 0)
    off2 = (b - p).astype(jnp.float32)
    off2 = off2 * off2
    j = lax.rem(own - h + ratio, ratio)
    for u in range(quarters):
        s = lax.rem(source - u + quarters, quarters)
        cut = slice(u * wide, (u + 1) * wide)
        squared = off2 + sq_ref[0, cut][None, None]
        o_ref[0, :, :, cut] = total[:, :, cut] + r_ref[s, j, 0] - diffusion * squared * w_ref[u, 0]


def params():
    return pltpu.CompilerParams(vmem_limit_bytes=VMEM)


def on_device(n_row, n_col, density, potential):
    width, window = density.shape[4], density.shape[2]
    cols, rows = density.shape[1], density.shape[3]
    ratio = n_row // n_col
    tall = up8(rows)
    lanes = window * window
    group = LANES // window
    groups = window // group
    quarters = n_col
    wide = lanes // quarters
    row, col = lax.axis_index("row"), lax.axis_index("col")
    zone, own = row // ratio, row % ratio
    kinetic, slope = operators(width)
    f32 = jnp.float32

    weights = np.zeros((window, width, 2 * LANES))
    eyes = np.zeros((group, width, LANES))
    e = np.arange(window)
    for q in range(window):
        at = (q % group) * window
        weights[q, :, at : at + window] = kinetic[:window].T
        weights[q, :, LANES + at : LANES + at + window] = -friction * (e - q)[None, :] * slope[:window].T
        if q < group:
            eyes[q, e, at + e] = 1.0
    whigh, wlow = split_host(weights)
    eye = jnp.asarray(eyes.astype(jnp.bfloat16))
    tiled = jnp.tile(potential[:, :window], (1, group))

    per = max(1, LANES // wide)
    unit = min(wide, LANES)
    store = max(wide, LANES)
    stores = lanes // store
    inner = store // LANES
    w_all, l_all = pl.pallas_call(
        functools.partial(first_kernel, group, rows),
        grid=(ratio, groups),
        in_specs=[
            pl.BlockSpec((2, rows, group, rows, width), lambda h, m: (0, h, m, 0, 0)),
            pl.BlockSpec((rows, LANES), lambda h, m: (0, 0)),
            pl.BlockSpec((group, width, 2 * LANES), lambda h, m: (m, 0, 0)),
            pl.BlockSpec((group, width, 2 * LANES), lambda h, m: (m, 0, 0)),
            pl.BlockSpec((group, width, LANES), lambda h, m: (0, 0, 0)),
        ],
        out_specs=[
            pl.BlockSpec((1, 2, rows, rows, LANES), lambda h, m: (m // inner, 0, h, 0, m % inner)),
            pl.BlockSpec((2, rows, rows, LANES), lambda h, m: (0, h, 0, m)),
        ],
        out_shape=[
            jax.ShapeDtypeStruct((stores, 2, cols, rows, store), f32),
            jax.ShapeDtypeStruct((2, cols, rows, lanes), f32),
        ],
        scratch_shapes=[pltpu.VMEM((rows, tall, width), f32)],
        compiler_params=params(),
        cost_estimate=pl.CostEstimate(flops=2 * 10**10, bytes_accessed=80 * 10**6, transcendentals=0),
        name="first_dimension",
    )(density, tiled, whigh, wlow, eye)
    if per > 1:
        w_all = jnp.moveaxis(w_all.reshape(stores, 2, cols, rows, per, wide), 4, 1).reshape(quarters, 2, cols, rows, wide)

    def permute(values, target):
        pairs = [(r * n_col + c, target(r, c)) for r in range(n_row) for c in range(n_col)]
        return lax.ppermute(values, ("row", "col"), pairs)

    def to_middle(j, k):
        return lambda r, c: (c * ratio + (r % ratio + j) % ratio) * n_col + (r // ratio + k) % n_col

    received = []
    for k in range(n_col):
        for j in range(ratio):
            piece = lax.dynamic_slice(
                w_all,
                ((zone + k) % n_col, 0, (own + j) % ratio * rows, 0, 0),
                (1, 2, rows, rows, wide),
            )[0]
            received.append(permute(piece, to_middle(j, k)))

    order = np.arange(lanes)
    perm = np.zeros((lanes, lanes), np.float32)
    perm[order, order % window * window + order // window] = 1.0
    perm = jnp.asarray(perm.astype(jnp.bfloat16))
    l_mirror = pl.pallas_call(
        functools.partial(mirror_kernel, rows),
        grid=(2, ratio),
        in_specs=[
            pl.BlockSpec((1, rows, rows, lanes), lambda c, h: (c, h, 0, 0)),
            pl.BlockSpec((lanes, lanes), lambda c, h: (0, 0)),
        ],
        out_specs=pl.BlockSpec((quarters, 1, 1, rows, rows, wide), lambda c, h: (0, h, c, 0, 0, 0)),
        out_shape=jax.ShapeDtypeStruct((quarters, ratio, 2, rows, rows, wide), f32),
        scratch_shapes=[pltpu.VMEM((rows, tall, lanes), f32), pltpu.VMEM((8, 128), f32)],
        compiler_params=params(),
        cost_estimate=pl.CostEstimate(flops=2 * 10**10, bytes_accessed=16 * 10**6, transcendentals=0),
        name="mirror_first",
    )(l_all, perm)

    pieces = n_row
    blocks = np.zeros((pieces, tall, 2, pieces, tall))
    for t, m in enumerate((kinetic, slope)):
        cut = m.reshape(pieces, rows, pieces, rows)
        blocks[:, :rows, t, :, :rows] = cut.transpose(2, 3, 0, 1)
    mhigh, mlow = split_host(blocks.reshape(pieces, tall, 2 * pieces * tall))
    sources = [
        (col - k + n_col) % n_col * ratio + (own - j + ratio) % ratio
        for k in range(n_col)
        for j in range(ratio)
    ]

    def arrange(m):
        picked = [lax.dynamic_index_in_dim(m, s, 0, keepdims=False) for s in sources]
        return jnp.concatenate(picked, axis=0).T

    l_second = pl.pallas_call(
        functools.partial(second_kernel, pieces, rows, tall),
        grid=(rows,),
        in_specs=[pl.BlockSpec(memory_space=pltpu.SMEM)]
        + [pl.BlockSpec((2, 1, rows, wide), lambda p: (0, p, 0, 0))] * pieces
        + [pl.BlockSpec((2 * pieces * tall, pieces * tall), lambda p: (0, 0))] * 2,
        out_specs=pl.BlockSpec((pieces, 2, 1, rows, wide), lambda p: (0, 0, p, 0, 0)),
        out_shape=jax.ShapeDtypeStruct((pieces, 2, rows, rows, wide), f32),
        scratch_shapes=[pltpu.VMEM((2, pieces * tall, wide), f32)],
        compiler_params=params(),
        name="second_dimension",
    )((row * rows).astype(jnp.int32).reshape(1), *received, arrange(mhigh), arrange(mlow))

    mine, arrived = [], []
    for s in range(n_col):
        piece = lax.dynamic_slice_in_dim(l_second, (col + s) % n_col * ratio, ratio, 0)
        if s > 0:
            piece = permute(piece, lambda r, c, s=s: r * n_col + (c + s) % n_col)
        half = piece + lax.dynamic_index_in_dim(l_mirror, (col - s + n_col) % n_col, 0, keepdims=False)
        mine.append(half)
        for j in range(ratio):
            out = lax.dynamic_index_in_dim(half, (own + j) % ratio, 0, keepdims=False)
            arrived.append(
                permute(out, lambda r, c, j=j: (c * ratio + (r % ratio + j) % ratio) * n_col + r // ratio)
            )
    mine = jnp.stack(mine)
    arrived = jnp.stack(arrived).reshape(n_col, ratio, 2, rows, rows, wide)

    where = jnp.stack([col, zone, own, row * rows, col * cols]).astype(jnp.int32)
    sq = ((order % window - order // window) ** 2).astype(np.float32).reshape(1, lanes)
    out = pl.pallas_call(
        functools.partial(last_kernel, quarters, ratio, rows, window),
        grid=(2, ratio),
        in_specs=[
            pl.BlockSpec(memory_space=pltpu.SMEM),
            pl.BlockSpec((n_col, 1, 1, rows, rows, wide), lambda c, h: (0, h, c, 0, 0, 0)),
            pl.BlockSpec((n_col, ratio, 1, rows, rows, wide), lambda c, h: (0, 0, c, 0, 0, 0)),
            pl.BlockSpec((quarters, 1, rows, rows, wide), lambda c, h: (0, c, h, 0, 0)),
            pl.BlockSpec((lanes, lanes), lambda c, h: (0, 0)),
            pl.BlockSpec((1, lanes), lambda c, h: (0, 0)),
        ],
        out_specs=pl.BlockSpec((1, rows, rows, lanes), lambda c, h: (c, h, 0, 0)),
        out_shape=jax.ShapeDtypeStruct((2, cols, rows, lanes), f32),
        scratch_shapes=[pltpu.VMEM((rows, tall, wide), f32)],
        compiler_params=params(),
        name="combine",
    )(where, mine, arrived, w_all, perm, jnp.asarray(sq))
    return out


def solution(mesh):
    body = functools.partial(on_device, mesh.shape["row"], mesh.shape["col"])
    in_specs = (P(None, "col", None, "row", None), P("row", None))
    out_specs = P(None, "col", "row", None)
    return jax.shard_map(
        body, mesh=mesh, in_specs=in_specs, out_specs=out_specs, check_vma=False
    )
```

```python
import functools

import jax
import jax.numpy as jnp
import numpy as np
from jax import lax
from jax.experimental import pallas as pl
from jax.experimental.pallas import tpu as pltpu
from jax.sharding import PartitionSpec as P

friction = 0.005
diffusion = 0.0001
LANES = 128
VMEM = 56 * 2**20


def operators(grid_width):
    n = np.arange(grid_width)
    wave = 2.0 * np.pi * np.fft.fftfreq(grid_width)
    slope_wave = np.where(n == grid_width // 2, 0.0, wave)
    angles = 2.0 * np.pi / grid_width * (n[:, None] * n[None, :] % grid_width)
    kinetic_row = (0.5 * wave * wave * np.cos(angles)).sum(1) / grid_width
    slope_row = -(slope_wave * np.sin(angles)).sum(1) / grid_width
    distance = (n[:, None] - n[None, :]) % grid_width
    return kinetic_row[distance], slope_row[distance]


def split_host(matrix):
    high = matrix.astype(np.float32).astype(jnp.bfloat16)
    low = (matrix - high.astype(np.float64)).astype(np.float32).astype(jnp.bfloat16)
    return jnp.asarray(high), jnp.asarray(low)


def split(values):
    high = values.astype(jnp.bfloat16)
    return high, (values - high.astype(jnp.float32)).astype(jnp.bfloat16)


def dot(a, b):
    return jnp.dot(a, b, preferred_element_type=jnp.float32)


def up8(n):
    return (n + 7) // 8 * 8


def first_kernel(group, rows, d_ref, v_ref, high_ref, low_ref, eye_ref, l_ref, pad):
    blocks, tall = pad.shape[0], pad.shape[1]

    @pl.when((pl.program_id(0) == 0) & (pl.program_id(1) == 0))
    def _():
        pad[...] = jnp.zeros_like(pad)

    window, mixed = [], []
    for c in range(2):
        win = jnp.zeros((blocks * tall, LANES), jnp.float32)
        mix = jnp.zeros((blocks * tall, 2 * LANES), jnp.float32)
        for q in range(group):
            pad[:, :rows, :] = d_ref[c, :, q]
            high, low = split(pad[...].reshape(blocks * tall, pad.shape[2]))
            mix += dot(high, high_ref[q]) + dot(low, high_ref[q]) + dot(high, low_ref[q])
            win += dot(high, eye_ref[q]) + dot(low, eye_ref[q])
        window.append(win.reshape(blocks, tall, LANES)[:, :rows])
        mixed.append(mix.reshape(blocks, tall, 2 * LANES)[:, :rows])
    v = v_ref[...][None]
    l_ref[0] = mixed[1][..., :LANES] + mixed[0][..., LANES:] + v * window[1]
    l_ref[1] = mixed[1][..., LANES:] - mixed[0][..., :LANES] - v * window[0]


def mirror_kernel(rows, l_ref, perm_ref, o_ref, pad, back):
    sign = 1.0 - 2.0 * pl.program_id(0).astype(jnp.float32)
    tall, lanes = pad.shape[1], pad.shape[2]
    quarters, wide = o_ref.shape[0], o_ref.shape[5]
    pad[...] = jnp.zeros_like(pad)
    for b in range(rows):
        pad[b, :rows, :] = l_ref[0, :, b, :]
    high, low = split(pad[...].reshape(rows * tall, lanes) * sign)
    for u in range(quarters):
        part = perm_ref[:, u * wide : (u + 1) * wide]
        out = dot(high, part) + dot(low, part)
        o_ref[u, 0, 0] = out.reshape(rows, tall, wide)[:, :rows]


def second_kernel(pieces, rows, tall, start_ref, *refs):
    parts = refs[:pieces]
    high_ref, low_ref, o_ref, pad = refs[pieces:]
    wide = pad.shape[2]

    @pl.when(pl.program_id(0) == 0)
    def _():
        pad[...] = jnp.zeros_like(pad)

    column = (start_ref[0] + pl.program_id(0)).astype(jnp.float32)
    out = []
    for c in range(2):
        for k in range(pieces):
            pad[c, k * tall : k * tall + rows, :] = parts[k][c, 0]
        high, low = split(pad[c])
        out.append(dot(high_ref[...], high) + dot(high_ref[...], low) + dot(low_ref[...], high))
    half = pieces * tall
    at = lax.broadcasted_iota(jnp.int32, (tall, wide), 0).astype(jnp.float32) - column
    for r in range(pieces):
        here = slice(r * tall, (r + 1) * tall)
        there = slice(half + r * tall, half + (r + 1) * tall)
        offset = friction * (at + float(r * rows))
        o_ref[r, 0, 0] = (out[1][here] - offset * out[0][there])[:rows]
        o_ref[r, 1, 0] = (-out[0][here] - offset * out[1][there])[:rows]


def last_kernel(quarters, ratio, rows, window, where_ref, y_ref, r_ref, w_ref, perm_ref, sq_ref, o_ref, pad):
    c, h = pl.program_id(0), pl.program_id(1)
    col, source, own, row_start, col_start = (where_ref[k] for k in range(5))
    sign = 1.0 - 2.0 * c.astype(jnp.float32)
    tall, wide = pad.shape[1], pad.shape[2]
    lanes = o_ref.shape[3]
    pad[...] = jnp.zeros_like(pad)
    total = jnp.zeros((rows * tall, lanes), jnp.float32)
    for u in range(quarters):
        s = lax.rem(col - u + quarters, quarters)
        for p in range(rows):
            pad[p, :rows, :] = y_ref[s, 0, 0, :, p, :]
        high, low = split(pad[...].reshape(rows * tall, wide) * sign)
        part = perm_ref[u * wide : (u + 1) * wide, :]
        total += dot(high, part) + dot(low, part)
    total = total.reshape(rows, tall, lanes)[:, :rows]
    b = row_start + lax.broadcasted_iota(jnp.int32, (rows, rows, 1), 1)
    p = col_start + h * rows + lax.broadcasted_iota(jnp.int32, (rows, rows, 1), 0)
    off2 = (b - p).astype(jnp.float32)
    off2 = off2 * off2
    j = lax.rem(own - h + ratio, ratio)
    for u in range(quarters):
        s = lax.rem(source - u + quarters, quarters)
        cut = slice(u * wide, (u + 1) * wide)
        squared = off2 + sq_ref[0, cut][None, None]
        o_ref[0, :, :, cut] = total[:, :, cut] + r_ref[s, j, 0] - diffusion * squared * w_ref[u, 0]


def params():
    return pltpu.CompilerParams(vmem_limit_bytes=VMEM)


def on_device(n_row, n_col, density, potential):
    width, window = density.shape[4], density.shape[2]
    cols, rows = density.shape[1], density.shape[3]
    ratio = n_row // n_col
    tall = up8(rows)
    lanes = window * window
    group = LANES // window
    groups = window // group
    quarters = n_col
    wide = lanes // quarters
    row, col = lax.axis_index("row"), lax.axis_index("col")
    zone, own = row // ratio, row % ratio
    kinetic, slope = operators(width)
    f32 = jnp.float32

    weights = np.zeros((window, width, 2 * LANES))
    eyes = np.zeros((group, width, LANES))
    e = np.arange(window)
    for q in range(window):
        at = (q % group) * window
        weights[q, :, at : at + window] = kinetic[:window].T
        weights[q, :, LANES + at : LANES + at + window] = -friction * (e - q)[None, :] * slope[:window].T
        if q < group:
            eyes[q, e, at + e] = 1.0
    taken = jnp.transpose(density[..., :window], (0, 1, 3, 2, 4))
    per = window // quarters
    w_all = jnp.stack(
        [
            taken[:, :, :, u * per : (u + 1) * per].reshape(2, cols, rows, wide)
            for u in range(quarters)
        ]
    )
    whigh, wlow = split_host(weights)
    eye = jnp.asarray(eyes.astype(jnp.bfloat16))
    tiled = jnp.tile(potential[:, :window], (1, group))

    l_all, = pl.pallas_call(
        functools.partial(first_kernel, group, rows),
        grid=(ratio, groups),
        in_specs=[
            pl.BlockSpec((2, rows, group, rows, width), lambda h, m: (0, h, m, 0, 0)),
            pl.BlockSpec((rows, LANES), lambda h, m: (0, 0)),
            pl.BlockSpec((group, width, 2 * LANES), lambda h, m: (m, 0, 0)),
            pl.BlockSpec((group, width, 2 * LANES), lambda h, m: (m, 0, 0)),
            pl.BlockSpec((group, width, LANES), lambda h, m: (0, 0, 0)),
        ],
        out_specs=[
            pl.BlockSpec((2, rows, rows, LANES), lambda h, m: (0, h, 0, m)),
        ],
        out_shape=[
            jax.ShapeDtypeStruct((2, cols, rows, lanes), f32),
        ],
        scratch_shapes=[pltpu.VMEM((rows, tall, width), f32)],
        compiler_params=params(),
        cost_estimate=pl.CostEstimate(flops=2 * 10**10, bytes_accessed=80 * 10**6, transcendentals=0),
        name="first_dimension",
    )(density, tiled, whigh, wlow, eye)
    def permute(values, target):
        pairs = [(r * n_col + c, target(r, c)) for r in range(n_row) for c in range(n_col)]
        return lax.ppermute(values, ("row", "col"), pairs)

    def to_middle(j, k):
        return lambda r, c: (c * ratio + (r % ratio + j) % ratio) * n_col + (r // ratio + k) % n_col

    received = []
    for k in range(n_col):
        for j in range(ratio):
            piece = lax.dynamic_slice(
                w_all,
                ((zone + k) % n_col, 0, (own + j) % ratio * rows, 0, 0),
                (1, 2, rows, rows, wide),
            )[0]
            received.append(permute(piece, to_middle(j, k)))

    order = np.arange(lanes)
    perm = np.zeros((lanes, lanes), np.float32)
    perm[order, order % window * window + order // window] = 1.0
    perm = jnp.asarray(perm.astype(jnp.bfloat16))
    l_mirror = pl.pallas_call(
        functools.partial(mirror_kernel, rows),
        grid=(2, ratio),
        in_specs=[
            pl.BlockSpec((1, rows, rows, lanes), lambda c, h: (c, h, 0, 0)),
            pl.BlockSpec((lanes, lanes), lambda c, h: (0, 0)),
        ],
        out_specs=pl.BlockSpec((quarters, 1, 1, rows, rows, wide), lambda c, h: (0, h, c, 0, 0, 0)),
        out_shape=jax.ShapeDtypeStruct((quarters, ratio, 2, rows, rows, wide), f32),
        scratch_shapes=[pltpu.VMEM((rows, tall, lanes), f32), pltpu.VMEM((8, 128), f32)],
        compiler_params=params(),
        cost_estimate=pl.CostEstimate(flops=2 * 10**10, bytes_accessed=16 * 10**6, transcendentals=0),
        name="mirror_first",
    )(l_all, perm)

    pieces = n_row
    blocks = np.zeros((pieces, tall, 2, pieces, tall))
    for t, m in enumerate((kinetic, slope)):
        cut = m.reshape(pieces, rows, pieces, rows)
        blocks[:, :rows, t, :, :rows] = cut.transpose(2, 3, 0, 1)
    mhigh, mlow = split_host(blocks.reshape(pieces, tall, 2 * pieces * tall))
    sources = [
        (col - k + n_col) % n_col * ratio + (own - j + ratio) % ratio
        for k in range(n_col)
        for j in range(ratio)
    ]

    def arrange(m):
        picked = [lax.dynamic_index_in_dim(m, s, 0, keepdims=False) for s in sources]
        return jnp.concatenate(picked, axis=0).T

    l_second = pl.pallas_call(
        functools.partial(second_kernel, pieces, rows, tall),
        grid=(rows,),
        in_specs=[pl.BlockSpec(memory_space=pltpu.SMEM)]
        + [pl.BlockSpec((2, 1, rows, wide), lambda p: (0, p, 0, 0))] * pieces
        + [pl.BlockSpec((2 * pieces * tall, pieces * tall), lambda p: (0, 0))] * 2,
        out_specs=pl.BlockSpec((pieces, 2, 1, rows, wide), lambda p: (0, 0, p, 0, 0)),
        out_shape=jax.ShapeDtypeStruct((pieces, 2, rows, rows, wide), f32),
        scratch_shapes=[pltpu.VMEM((2, pieces * tall, wide), f32)],
        compiler_params=params(),
        name="second_dimension",
    )((row * rows).astype(jnp.int32).reshape(1), *received, arrange(mhigh), arrange(mlow))

    mine, arrived = [], []
    for s in range(n_col):
        piece = lax.dynamic_slice_in_dim(l_second, (col + s) % n_col * ratio, ratio, 0)
        if s > 0:
            piece = permute(piece, lambda r, c, s=s: r * n_col + (c + s) % n_col)
        half = piece + lax.dynamic_index_in_dim(l_mirror, (col - s + n_col) % n_col, 0, keepdims=False)
        mine.append(half)
        for j in range(ratio):
            out = lax.dynamic_index_in_dim(half, (own + j) % ratio, 0, keepdims=False)
            arrived.append(
                permute(out, lambda r, c, j=j: (c * ratio + (r % ratio + j) % ratio) * n_col + r // ratio)
            )
    mine = jnp.stack(mine)
    arrived = jnp.stack(arrived).reshape(n_col, ratio, 2, rows, rows, wide)

    where = jnp.stack([col, zone, own, row * rows, col * cols]).astype(jnp.int32)
    sq = ((order % window - order // window) ** 2).astype(np.float32).reshape(1, lanes)
    out = pl.pallas_call(
        functools.partial(last_kernel, quarters, ratio, rows, window),
        grid=(2, ratio),
        in_specs=[
            pl.BlockSpec(memory_space=pltpu.SMEM),
            pl.BlockSpec((n_col, 1, 1, rows, rows, wide), lambda c, h: (0, h, c, 0, 0, 0)),
            pl.BlockSpec((n_col, ratio, 1, rows, rows, wide), lambda c, h: (0, 0, c, 0, 0, 0)),
            pl.BlockSpec((quarters, 1, rows, rows, wide), lambda c, h: (0, c, h, 0, 0)),
            pl.BlockSpec((lanes, lanes), lambda c, h: (0, 0)),
            pl.BlockSpec((1, lanes), lambda c, h: (0, 0)),
        ],
        out_specs=pl.BlockSpec((1, rows, rows, lanes), lambda c, h: (c, h, 0, 0)),
        out_shape=jax.ShapeDtypeStruct((2, cols, rows, lanes), f32),
        scratch_shapes=[pltpu.VMEM((rows, tall, wide), f32)],
        compiler_params=params(),
        name="combine",
    )(where, mine, arrived, w_all, perm, jnp.asarray(sq))
    return out


def solution(mesh):
    body = functools.partial(on_device, mesh.shape["row"], mesh.shape["col"])
    in_specs = (P(None, "col", None, "row", None), P("row", None))
    out_specs = P(None, "col", "row", None)
    return jax.shard_map(
        body, mesh=mesh, in_specs=in_specs, out_specs=out_specs, check_vma=False
    )
```

```python
import functools

import jax
import jax.numpy as jnp
import numpy as np
from jax import lax
from jax.experimental import pallas as pl
from jax.experimental.pallas import tpu as pltpu
from jax.sharding import PartitionSpec as P

friction = 0.005
diffusion = 0.0001
LANES = 128
VMEM = 56 * 2**20


def operators(grid_width):
    n = np.arange(grid_width)
    wave = 2.0 * np.pi * np.fft.fftfreq(grid_width)
    slope_wave = np.where(n == grid_width // 2, 0.0, wave)
    angles = 2.0 * np.pi / grid_width * (n[:, None] * n[None, :] % grid_width)
    kinetic_row = (0.5 * wave * wave * np.cos(angles)).sum(1) / grid_width
    slope_row = -(slope_wave * np.sin(angles)).sum(1) / grid_width
    distance = (n[:, None] - n[None, :]) % grid_width
    return kinetic_row[distance], slope_row[distance]


def split_host(matrix):
    high = matrix.astype(np.float32).astype(jnp.bfloat16)
    low = (matrix - high.astype(np.float64)).astype(np.float32).astype(jnp.bfloat16)
    return jnp.asarray(high), jnp.asarray(low)


def split(values):
    high = values.astype(jnp.bfloat16)
    return high, (values - high.astype(jnp.float32)).astype(jnp.bfloat16)


def dot(a, b):
    return jnp.dot(a, b, preferred_element_type=jnp.float32)


def up8(n):
    return (n + 7) // 8 * 8


def first_kernel(group, rows, d_ref, v_ref, high_ref, low_ref, eye_ref, l_ref, pad):
    blocks, tall = pad.shape[0], pad.shape[1]

    @pl.when((pl.program_id(0) == 0) & (pl.program_id(1) == 0))
    def _():
        pad[...] = jnp.zeros_like(pad)

    window, mixed = [], []
    for c in range(2):
        win = jnp.zeros((blocks * tall, LANES), jnp.float32)
        mix = jnp.zeros((blocks * tall, 2 * LANES), jnp.float32)
        for q in range(group):
            pad[:, :rows, :] = d_ref[c, :, q]
            high, low = split(pad[...].reshape(blocks * tall, pad.shape[2]))
            mix += dot(high, high_ref[q]) + dot(low, high_ref[q]) + dot(high, low_ref[q])
            win += dot(high, eye_ref[q]) + dot(low, eye_ref[q])
        window.append(win.reshape(blocks, tall, LANES)[:, :rows])
        mixed.append(mix.reshape(blocks, tall, 2 * LANES)[:, :rows])
    v = v_ref[...][None]
    l_ref[0] = mixed[1][..., :LANES] + mixed[0][..., LANES:] + v * window[1]
    l_ref[1] = mixed[1][..., LANES:] - mixed[0][..., :LANES] - v * window[0]


def mirror_kernel(rows, l_ref, perm_ref, o_ref, pad, back):
    sign = 1.0 - 2.0 * pl.program_id(0).astype(jnp.float32)
    tall, lanes = pad.shape[1], pad.shape[2]
    quarters, wide = o_ref.shape[0], o_ref.shape[5]
    pad[...] = jnp.zeros_like(pad)
    for b in range(rows):
        pad[b, :rows, :] = l_ref[0, :, b, :]
    high, low = split(pad[...].reshape(rows * tall, lanes) * sign)
    for u in range(quarters):
        part = perm_ref[:, u * wide : (u + 1) * wide]
        out = dot(high, part) + dot(low, part)
        o_ref[u, 0, 0] = out.reshape(rows, tall, wide)[:, :rows]


def second_kernel(pieces, rows, tall, start_ref, *refs):
    parts = refs[:pieces]
    high_ref, low_ref, o_ref, pad = refs[pieces:]
    wide = pad.shape[2]

    @pl.when(pl.program_id(0) == 0)
    def _():
        pad[...] = jnp.zeros_like(pad)

    column = (start_ref[0] + pl.program_id(0)).astype(jnp.float32)
    out = []
    for c in range(2):
        for k in range(pieces):
            pad[c, k * tall : k * tall + rows, :] = parts[k][c, 0]
        high, low = split(pad[c])
        out.append(dot(high_ref[...], high) + dot(high_ref[...], low) + dot(low_ref[...], high))
    half = pieces * tall
    at = lax.broadcasted_iota(jnp.int32, (tall, wide), 0).astype(jnp.float32) - column
    for r in range(pieces):
        here = slice(r * tall, (r + 1) * tall)
        there = slice(half + r * tall, half + (r + 1) * tall)
        offset = friction * (at + float(r * rows))
        o_ref[r, 0, 0] = (out[1][here] - offset * out[0][there])[:rows]
        o_ref[r, 1, 0] = (-out[0][here] - offset * out[1][there])[:rows]


def last_kernel(quarters, ratio, rows, window, where_ref, y_ref, r_ref, w_ref, perm_ref, sq_ref, o_ref, pad):
    c, h = pl.program_id(0), pl.program_id(1)
    col, source, own, row_start, col_start = (where_ref[k] for k in range(5))
    sign = 1.0 - 2.0 * c.astype(jnp.float32)
    tall, wide = pad.shape[1], pad.shape[2]
    lanes = o_ref.shape[3]
    pad[...] = jnp.zeros_like(pad)
    total = jnp.zeros((rows * tall, lanes), jnp.float32)
    for u in range(quarters):
        s = lax.rem(col - u + quarters, quarters)
        for p in range(rows):
            pad[p, :rows, :] = y_ref[s, 0, 0, :, p, :]
        high, low = split(pad[...].reshape(rows * tall, wide) * sign)
        part = perm_ref[u * wide : (u + 1) * wide, :]
        total += dot(high, part) + dot(low, part)
    total = total.reshape(rows, tall, lanes)[:, :rows]
    b = row_start + lax.broadcasted_iota(jnp.int32, (rows, rows, 1), 1)
    p = col_start + h * rows + lax.broadcasted_iota(jnp.int32, (rows, rows, 1), 0)
    off2 = (b - p).astype(jnp.float32)
    off2 = off2 * off2
    j = lax.rem(own - h + ratio, ratio)
    for u in range(quarters):
        s = lax.rem(source - u + quarters, quarters)
        cut = slice(u * wide, (u + 1) * wide)
        squared = off2 + sq_ref[0, cut][None, None]
        o_ref[0, :, :, cut] = total[:, :, cut] + r_ref[s, j, 0] - diffusion * squared * w_ref[u, 0]


def params():
    return pltpu.CompilerParams(vmem_limit_bytes=VMEM)


def on_device(n_row, n_col, density, potential):
    width, window = density.shape[4], density.shape[2]
    cols, rows = density.shape[1], density.shape[3]
    ratio = n_row // n_col
    tall = up8(rows)
    lanes = window * window
    group = LANES // window
    groups = window // group
    quarters = n_col
    wide = lanes // quarters
    row, col = lax.axis_index("row"), lax.axis_index("col")
    zone, own = row // ratio, row % ratio
    kinetic, slope = operators(width)
    f32 = jnp.float32

    weights = np.zeros((window, width, 2 * LANES))
    eyes = np.zeros((group, width, LANES))
    e = np.arange(window)
    for q in range(window):
        at = (q % group) * window
        weights[q, :, at : at + window] = kinetic[:window].T
        weights[q, :, LANES + at : LANES + at + window] = -friction * (e - q)[None, :] * slope[:window].T
        if q < group:
            eyes[q, e, at + e] = 1.0
    taken = jnp.transpose(density[..., :window], (0, 1, 3, 2, 4))
    per = window // quarters
    w_all = jnp.stack(
        [
            taken[:, :, :, u * per : (u + 1) * per].reshape(2, cols, rows, wide)
            for u in range(quarters)
        ]
    )
    whigh, wlow = split_host(weights)
    eye = jnp.asarray(eyes.astype(jnp.bfloat16))
    tiled = jnp.tile(potential[:, :window], (1, group))

    l_all, = pl.pallas_call(
        functools.partial(first_kernel, group, rows),
        grid=(ratio, groups),
        in_specs=[
            pl.BlockSpec((2, rows, group, rows, width), lambda h, m: (0, h, m, 0, 0)),
            pl.BlockSpec((rows, LANES), lambda h, m: (0, 0)),
            pl.BlockSpec((group, width, 2 * LANES), lambda h, m: (m, 0, 0)),
            pl.BlockSpec((group, width, 2 * LANES), lambda h, m: (m, 0, 0)),
            pl.BlockSpec((group, width, LANES), lambda h, m: (0, 0, 0)),
        ],
        out_specs=[
            pl.BlockSpec((2, rows, rows, LANES), lambda h, m: (0, h, 0, m)),
        ],
        out_shape=[
            jax.ShapeDtypeStruct((2, cols, rows, lanes), f32),
        ],
        scratch_shapes=[pltpu.VMEM((rows, tall, width), f32)],
        compiler_params=params(),
        cost_estimate=pl.CostEstimate(flops=2 * 10**10, bytes_accessed=80 * 10**6, transcendentals=0),
        name="first_dimension",
    )(density, tiled, whigh, wlow, eye)
    def permute(values, target):
        pairs = [(r * n_col + c, target(r, c)) for r in range(n_row) for c in range(n_col)]
        return lax.ppermute(values, ("row", "col"), pairs)

    def swap(values, target, early):
        half = n_col // 2
        direct, first, last = [], [], []
        for r in range(n_row):
            for c in range(n_col):
                to_r, to_c = target(r, c)
                here, there = r * n_col + c, to_r * n_col + to_c
                if c // half == to_c // half:
                    direct.append((here, there))
                    continue
                via = r * n_col + (c + half) % n_col if early else to_r * n_col + (to_c + half) % n_col
                first.append((here, via))
                last.append((via, there))
        axes = ("row", "col")
        moved = lax.ppermute(lax.ppermute(values, axes, first), axes, last)
        return moved + lax.ppermute(values, axes, direct)

    def to_middle(j, k):
        return lambda r, c: (c * ratio + (r % ratio + j) % ratio) * n_col + (r // ratio + k) % n_col

    received = []
    for k in range(n_col):
        for j in range(ratio):
            piece = lax.dynamic_slice(
                w_all,
                ((zone + k) % n_col, 0, (own + j) % ratio * rows, 0, 0),
                (1, 2, rows, rows, wide),
            )[0]
            received.append(permute(piece, to_middle(j, k)))

    order = np.arange(lanes)
    perm = np.zeros((lanes, lanes), np.float32)
    perm[order, order % window * window + order // window] = 1.0
    perm = jnp.asarray(perm.astype(jnp.bfloat16))
    l_mirror = pl.pallas_call(
        functools.partial(mirror_kernel, rows),
        grid=(2, ratio),
        in_specs=[
            pl.BlockSpec((1, rows, rows, lanes), lambda c, h: (c, h, 0, 0)),
            pl.BlockSpec((lanes, lanes), lambda c, h: (0, 0)),
        ],
        out_specs=pl.BlockSpec((quarters, 1, 1, rows, rows, wide), lambda c, h: (0, h, c, 0, 0, 0)),
        out_shape=jax.ShapeDtypeStruct((quarters, ratio, 2, rows, rows, wide), f32),
        scratch_shapes=[pltpu.VMEM((rows, tall, lanes), f32), pltpu.VMEM((8, 128), f32)],
        compiler_params=params(),
        cost_estimate=pl.CostEstimate(flops=2 * 10**10, bytes_accessed=16 * 10**6, transcendentals=0),
        name="mirror_first",
    )(l_all, perm)

    pieces = n_row
    blocks = np.zeros((pieces, tall, 2, pieces, tall))
    for t, m in enumerate((kinetic, slope)):
        cut = m.reshape(pieces, rows, pieces, rows)
        blocks[:, :rows, t, :, :rows] = cut.transpose(2, 3, 0, 1)
    mhigh, mlow = split_host(blocks.reshape(pieces, tall, 2 * pieces * tall))
    sources = [
        (col - k + n_col) % n_col * ratio + (own - j + ratio) % ratio
        for k in range(n_col)
        for j in range(ratio)
    ]

    def arrange(m):
        picked = [lax.dynamic_index_in_dim(m, s, 0, keepdims=False) for s in sources]
        return jnp.concatenate(picked, axis=0).T

    l_second = pl.pallas_call(
        functools.partial(second_kernel, pieces, rows, tall),
        grid=(rows,),
        in_specs=[pl.BlockSpec(memory_space=pltpu.SMEM)]
        + [pl.BlockSpec((2, 1, rows, wide), lambda p: (0, p, 0, 0))] * pieces
        + [pl.BlockSpec((2 * pieces * tall, pieces * tall), lambda p: (0, 0))] * 2,
        out_specs=pl.BlockSpec((pieces, 2, 1, rows, wide), lambda p: (0, 0, p, 0, 0)),
        out_shape=jax.ShapeDtypeStruct((pieces, 2, rows, rows, wide), f32),
        scratch_shapes=[pltpu.VMEM((2, pieces * tall, wide), f32)],
        compiler_params=params(),
        name="second_dimension",
    )((row * rows).astype(jnp.int32).reshape(1), *received, arrange(mhigh), arrange(mlow))

    mine, arrived = [], []
    for s in range(n_col):
        piece = lax.dynamic_slice_in_dim(l_second, (col + s) % n_col * ratio, ratio, 0)
        if s > 0:
            piece = permute(piece, lambda r, c, s=s: r * n_col + (c + s) % n_col)
        half = piece + lax.dynamic_index_in_dim(l_mirror, (col - s + n_col) % n_col, 0, keepdims=False)
        mine.append(half)
        for j in range(ratio):
            out = lax.dynamic_index_in_dim(half, (own + j) % ratio, 0, keepdims=False)
            arrived.append(
                swap(out, lambda r, c, j=j: (c * ratio + (r % ratio + j) % ratio, r // ratio), j % 2 == 0)
            )
    mine = jnp.stack(mine)
    arrived = jnp.stack(arrived).reshape(n_col, ratio, 2, rows, rows, wide)

    where = jnp.stack([col, zone, own, row * rows, col * cols]).astype(jnp.int32)
    sq = ((order % window - order // window) ** 2).astype(np.float32).reshape(1, lanes)
    out = pl.pallas_call(
        functools.partial(last_kernel, quarters, ratio, rows, window),
        grid=(2, ratio),
        in_specs=[
            pl.BlockSpec(memory_space=pltpu.SMEM),
            pl.BlockSpec((n_col, 1, 1, rows, rows, wide), lambda c, h: (0, h, c, 0, 0, 0)),
            pl.BlockSpec((n_col, ratio, 1, rows, rows, wide), lambda c, h: (0, 0, c, 0, 0, 0)),
            pl.BlockSpec((quarters, 1, rows, rows, wide), lambda c, h: (0, c, h, 0, 0)),
            pl.BlockSpec((lanes, lanes), lambda c, h: (0, 0)),
            pl.BlockSpec((1, lanes), lambda c, h: (0, 0)),
        ],
        out_specs=pl.BlockSpec((1, rows, rows, lanes), lambda c, h: (c, h, 0, 0)),
        out_shape=jax.ShapeDtypeStruct((2, cols, rows, lanes), f32),
        scratch_shapes=[pltpu.VMEM((rows, tall, wide), f32)],
        compiler_params=params(),
        name="combine",
    )(where, mine, arrived, w_all, perm, jnp.asarray(sq))
    return out


def solution(mesh):
    body = functools.partial(on_device, mesh.shape["row"], mesh.shape["col"])
    in_specs = (P(None, "col", None, "row", None), P("row", None))
    out_specs = P(None, "col", "row", None)
    return jax.shard_map(
        body, mesh=mesh, in_specs=in_specs, out_specs=out_specs, check_vma=False
    )
```
